32 devices in a mesh: lat: 4 (over y, core), lon: 8 (over z, x).
Axes of the slice: x: 2, y: 2, z: 4, core: 2. Of those that a mesh axis runs over, the one named last changes fastest.
Arguments:
- adjoint_in: float32 [4, 72, 32, 1024], P(None, None, 'lat', 'lon'), may hold values from -6 to 6
- wind_u: float32 [72, 32, 1024], P(None, 'lat', 'lon'), may hold values from -0.45 to 0.45
- wind_v: float32 [72, 32, 1024], P(None, 'lat', 'lon'), may hold values from -0.45 to 0.45
- diffusion: float32 [72, 32, 1024], P(None, 'lat', 'lon'), may hold values from 0.02 to 8
- kernel_rows: bfloat16 [72, 65536], P(None, ('lat', 'lon')), may hold values from 0 to 1
- retrieval_misfit: bfloat16 [4, 65536], P(None, ('lat', 'lon')), may hold values from -6 to 6
- retrieval_columns: int32 [65536], P(('lat', 'lon')), may hold values from 0 to 8191, as said below
- retrieval_counts: int32 [32], P(('lat', 'lon')), may hold values from 512 to 2048, as said below
- station_cells: int32 [512], P(('lat', 'lon')), may hold values from 0 to 1023
- station_misfit: float32 [4, 512], P(None, ('lat', 'lon')), may hold values from -6 to 6
Outputs:
- adjoint_out: float32 [4, 72, 32, 1024], P(None, None, 'lat', 'lon')
The draws below stay inside these ranges and needn't reach their ends.
Inputs may be any that keep to these rules, and one draw needn't show every extreme that they name: Only the first retrieval_counts slots of a device hold live retrievals; in each latitude band one device holds 2048. `retrieval_columns`: each value names a tile of the holding device's latitude band (value // 1024) and a cell of it (row times 128 plus column). Among the live retrievals of one device at most 512 name one tile, and in each band one tile is named by exactly 512 live retrievals of every device of the band.
All inputs are finite; a program needn't handle non-finite values.
Results may differ from the reference program's by a relative error of at most 0.0003.
Values may be sent and summed in bfloat16 or wider, within the bound.
A program may use at most 128 MiB of HBM per device.

```python
import math
import jax
import jax.numpy as jnp

NTR = 4
L = 72
CLAT = 8
CLON = 128
R_DEV = 2048
S_DEV = 16
COLS = 1024
CAP = 512
NLAT = 32
NLON = 1024
RETR = 65536
STATIONS = 512
N_LAT = 4
N_LON = 8


def band_layout(key):
    hot_key, count_key, order_key, cell_key = jax.random.split(key, 4)
    devices = N_LAT * N_LON
    hottest = jax.random.randint(hot_key, (N_LAT,), 0, N_LON)
    spread = jax.random.randint(count_key, (N_LAT, N_LON), 8, 33)
    busiest = (hottest + 1) % N_LON
    spread = jnp.where(jnp.arange(N_LON)[None, :] == busiest[:, None], 32, spread)
    counts = (CAP + (R_DEV - CAP) * spread * spread // 1024).reshape(devices)
    hot_tiles = jnp.repeat(hottest, N_LON)
    position = jnp.arange(R_DEV)

    def one_device(device_key, hot_tile, count):
        first_key, second_key, third_key = jax.random.split(device_key, 3)
        others = jax.random.permutation(first_key, N_LON - 1)
        cyclic = others[jnp.maximum(position - CAP, 0) % (N_LON - 1)]
        base = jnp.where(position < CAP, hot_tile, (hot_tile + 1 + cyclic) % N_LON)
        noise = jax.random.randint(second_key, (R_DEV,), 0, 4096)
        score = jnp.where(position < CAP, position, R_DEV + noise * R_DEV + position)
        mixed = base[jnp.argsort(score, stable=True)]
        noise_two = jax.random.randint(third_key, (R_DEV,), 0, 4096)
        score_two = jnp.where(position < count, noise_two * R_DEV + position, 4096 * R_DEV + position)
        return mixed[jnp.argsort(score_two, stable=True)]
    device_keys = jax.random.split(order_key, devices)
    tiles = jax.vmap(one_device)(device_keys, hot_tiles, counts)
    cells = jax.random.randint(cell_key, (devices, R_DEV), 0, CLAT * CLON)
    columns = (tiles * (CLAT * CLON) + cells).reshape(devices * R_DEV).astype(jnp.int32)
    return (columns, counts.astype(jnp.int32))


def draw_retrieval_columns(key, part):
    return band_layout(jax.random.fold_in(key, 11))[0]


def draw_retrieval_counts(key, part):
    return band_layout(jax.random.fold_in(key, 11))[1]


def touch_ends(values, rng, least, high):
    longest = values.shape.index(max(values.shape))
    spots = []
    for shift in (0, 1):
        where = [jax.random.randint(jax.random.fold_in(rng, axis), (), 0, length) for axis, length in enumerate(values.shape)]
        where[longest] = (where[longest] + shift) % values.shape[longest]
        spots.append(tuple(where))
    return values.at[spots[0]].set(least).at[spots[1]].set(high)


def level_of(rng, dims, cuts, least, high):
    loudness, own = 1.0, jax.random.fold_in(rng, 6)
    for dim, shards_of in cuts:
        heights = jnp.exp(jax.random.uniform(jax.random.fold_in(own, dim), (shards_of,), jnp.float32, least / len(cuts), high / len(cuts)))
        loudness = loudness * jnp.repeat(heights, dims[dim] // shards_of).reshape([-1 if axis == dim else 1 for axis in range(len(dims))])
    return loudness


def gaussian(own_key, dims, scale, bound, shards=(), kind=jnp.bfloat16):
    values = jax.random.normal(own_key, dims, jnp.float32) * scale
    if len(shards) > 0:
        values = level_of(own_key, dims, shards, -0.22, 0.18) * values
    return jnp.clip(values, min=-bound, max=bound).astype(kind)


def setup_inputs(seed: int = 0) -> dict:
    key_list = jax.random.split(jax.random.key(seed), 11)
    return {
        "adjoint_in": gaussian(key_list[0], (NTR, L, NLAT, NLON), 1.0, 6.0, ((2, 4), (3, 8)), jnp.float32),
        "wind_u": jnp.clip(jax.random.uniform(key_list[1], (L, NLAT, NLON), jnp.float32, -0.45, 0.45) * level_of(key_list[1], (L, NLAT, NLON), ((1, 4), (2, 8)), -0.4, 0.0), -0.45, 0.45),
        "wind_v": jnp.clip(jax.random.uniform(key_list[2], (L, NLAT, NLON), jnp.float32, -0.45, 0.45) * level_of(key_list[2], (L, NLAT, NLON), ((1, 4), (2, 8)), -0.4, 0.0), -0.45, 0.45),
        "diffusion": jnp.clip(jnp.exp(math.log(8.0) - 5.9914646 * jax.random.uniform(key_list[3], (L, NLAT, NLON), jnp.float32) ** level_of(key_list[3], (L, NLAT, NLON), ((1, 4), (2, 8)), -0.2, 0.2)), 0.02, 8.0),
        "kernel_rows": jnp.clip(1.0 * jax.random.uniform(key_list[4], (L, RETR), jnp.float32) ** level_of(key_list[4], (L, RETR), ((1, 32),), -0.2, 0.2), 0.0, 1.0).astype(jnp.bfloat16),
        "retrieval_misfit": gaussian(key_list[5], (NTR, RETR), 1.0, 6.0, ((1, 32),)),
        "retrieval_columns": draw_retrieval_columns(jax.random.fold_in(key_list[10], 71), 0),
        "retrieval_counts": draw_retrieval_counts(jax.random.fold_in(key_list[10], 71), 0),
        "station_cells": touch_ends(jax.random.randint(key_list[8], (STATIONS,), 0, COLS), jax.random.fold_in(key_list[8], 1), 0, COLS - 1).astype(jnp.int32),
        "station_misfit": gaussian(key_list[9], (NTR, STATIONS), 1.0, 6.0, ((1, 32),), jnp.float32),
    }


def pad_global(field):
    wide = jnp.pad(field, ((0, 0), (0, 0), (1, 1), (0, 0)))
    return jnp.concatenate([wide[..., -1:], wide, wide[..., :1]], axis=3)


def advect(padded, wind_u, wind_v):
    centre = padded[:, :, 1:-1, 1:-1]
    east = padded[:, :, 1:-1, 2:]
    west = padded[:, :, 1:-1, :-2]
    north = padded[:, :, 2:, 1:-1]
    south = padded[:, :, :-2, 1:-1]
    result = centre + jnp.maximum(wind_u, 0.0) * (east - centre)
    result = result + jnp.maximum(-wind_u, 0.0) * (west - centre)
    result = result + jnp.maximum(wind_v, 0.0) * (north - centre)
    result = result + jnp.maximum(-wind_v, 0.0) * (south - centre)
    return result


def factor(diffusion):
    levels = diffusion.shape[0]
    inverse = [1.0 / (1.0 + diffusion[0])]
    for level in range(1, levels):
        below = diffusion[level - 1]
        weight = 1.0 + below + diffusion[level] - below * below * inverse[level - 1]
        inverse.append(1.0 / weight)
    upper = [diffusion[level] * inverse[level] for level in range(levels - 1)]
    return inverse, upper


def relax(field, diffusion, inverse, upper):
    levels = diffusion.shape[0]
    sweep = [field[:, 0] * inverse[0]]
    for level in range(1, levels):
        sweep.append((field[:, level] + diffusion[level - 1] * sweep[-1]) * inverse[level])
    result = [sweep[-1]]
    for level in range(levels - 2, -1, -1):
        result.append(sweep[level] + upper[level] * result[-1])
    ordered = result[::-1]
    return jnp.stack(ordered, axis=1)


def advance(field, wind_u, wind_v, diffusion, inverse, upper):
    return relax(advect(pad_global(field), wind_u, wind_v), diffusion, inverse, upper)


def reference(adjoint_in, wind_u, wind_v, diffusion, kernel_rows, retrieval_misfit, retrieval_columns, retrieval_counts, station_cells, station_misfit):
    cells_total = NLAT * NLON
    holder = jnp.arange(STATIONS, dtype=jnp.int32) // S_DEV
    band = holder // N_LON
    tile = holder % N_LON
    row = band * CLAT + station_cells // CLON
    column = tile * CLON + station_cells % CLON
    place = (row * NLON + column).astype(jnp.int32)
    surface = jax.ops.segment_sum(station_misfit.T, place, num_segments=cells_total)
    started = adjoint_in.at[:, 0].add(surface.T.reshape(NTR, NLAT, NLON))
    inverse, upper = factor(diffusion)
    first = advance(started, wind_u, wind_v, diffusion, inverse, upper)
    slot = jnp.arange(RETR, dtype=jnp.int32)
    owner = slot // R_DEV
    live = (slot % R_DEV) < retrieval_counts[owner]
    rband = owner // N_LON
    rtile = retrieval_columns // COLS
    rcell = retrieval_columns % COLS
    rrow = rband * CLAT + rcell // CLON
    rcolumn = rtile * CLON + rcell % CLON
    rplace = (rrow * NLON + rcolumn).astype(jnp.int32)
    rows_wide = kernel_rows.astype(jnp.float32).T
    pieces = []
    for tracer in range(NTR):
        weight = jnp.where(live, retrieval_misfit[tracer].astype(jnp.float32), jnp.float32(0.0))
        summed = jax.ops.segment_sum(rows_wide * weight[:, None], rplace, num_segments=cells_total)
        pieces.append(summed.T.reshape(L, NLAT, NLON))
    injected = first + jnp.stack(pieces, axis=0)
    field = advance(injected, wind_u, wind_v, diffusion, inverse, upper)
    return advance(field, wind_u, wind_v, diffusion, inverse, upper)
```

```python
import functools

import jax
import jax.numpy as jnp
from jax import lax
from jax.experimental import pallas as pl
from jax.experimental.pallas import tpu as pltpu
from jax.sharding import PartitionSpec as P

MESH = pl.DeviceIdType.MESH
F32 = jnp.float32
BF16 = jnp.bfloat16
UNROLL = 8
PARTS = 3
NT = (((1,), (1,)), ((), ()))


def route_kernel(n_lon, cap, cols, lon_cells, count_ref, rows_ref, misfit_ref, column_ref, out_ref, pay_ref):
    levels, slots = rows_ref.shape
    tracers = misfit_ref.shape[0]
    width = out_ref.shape[2]
    column = column_ref[...]
    tile = column // cols
    cell = column - tile * cols
    lat_row = cell // lon_cells
    lane = cell - lat_row * lon_cells
    slot = lax.broadcasted_iota(jnp.int32, (1, slots), 1)
    live = slot < count_ref[0]
    tile = jnp.where(live, tile, -1)
    which = lax.broadcasted_iota(jnp.int32, (n_lon, slots), 0)
    hits = jnp.where(which == tile, 1.0, 0.0).astype(F32)
    step = 256
    before = (
        lax.broadcasted_iota(jnp.int32, (step, step), 0)
        < lax.broadcasted_iota(jnp.int32, (step, step), 1)
    )
    upper = jnp.where(before, 1.0, 0.0).astype(BF16)
    base = jnp.zeros((n_lon, 1), F32)
    codes = []
    for start in range(0, slots, step):
        part = hits[:, start : start + step]
        ahead = jnp.dot(part.astype(BF16), upper, preferred_element_type=F32) + base
        codes.append(jnp.sum(part * ahead, axis=0, keepdims=True))
        base = base + jnp.sum(part, axis=1, keepdims=True)
    rank = jnp.concatenate(codes, axis=1)
    place = jnp.where(live, tile.astype(F32) * cap + rank, -1.0)
    wide = rows_ref[...].astype(F32)
    pay_ref[0 : levels - 8, :] = wide[: levels - 8].astype(BF16)
    tail = jnp.concatenate(
        [
            misfit_ref[...].astype(F32),
            lat_row.astype(F32),
            lane.astype(F32),
            jnp.zeros((8 - tracers - 2, slots), F32),
        ],
        axis=0,
    )
    pay_ref[levels - 8 : levels + 8, :] = jnp.concatenate([wide[levels - 8 :], tail], axis=0).astype(BF16)
    index = lax.broadcasted_iota(jnp.int32, (width, slots), 0).astype(F32).astype(BF16)
    one = jnp.ones((width, slots), BF16)
    none = jnp.zeros((width, slots), BF16)

    def block(j, carry):
        local = jnp.clip(place - (j * width).astype(F32), -1.0, float(width))
        spread = jnp.broadcast_to(local.astype(BF16), (width, slots))
        pick = jnp.where(spread == index, one, none)
        out_ref[j] = lax.dot_general(
            pay_ref[...], pick, NT, preferred_element_type=F32
        ).astype(BF16)
        return carry

    lax.fori_loop(0, out_ref.shape[0], block, 0)


def transport_kernel(
    n_lat, n_lon,
    adj_ref, u_ref, v_ref, k_ref, packed_ref, cell_ref, misfit_ref,
    out_ref,
    field, y_buf, kpad, fac, acc, recv,
    row_out, row_in, col_out, col_in,
    route_send, route_recv, halo_send, halo_recv,
):
    tracers, levels = adj_ref.shape[:2]
    blocks = levels // UNROLL
    per_part = blocks // PARTS
    a = lax.axis_index("lat")
    b = lax.axis_index("lon")
    north, south = lax.rem(a + 1, n_lat), lax.rem(a + n_lat - 1, n_lat)
    east, west = lax.rem(b + 1, n_lon), lax.rem(b + n_lon - 1, n_lon)
    has_north, has_south = a < n_lat - 1, a > 0
    chunk = recv.shape[1]

    barrier = pltpu.get_barrier_semaphore()
    for other in (north, south):
        pl.semaphore_signal(barrier, inc=1, device_id=(other, b), device_id_type=MESH)

    def greet(o, carry):
        pl.semaphore_signal(
            barrier, inc=1, device_id=(a, lax.rem(b + o, n_lon)), device_id_type=MESH
        )
        return carry

    lax.fori_loop(1, n_lon, greet, 0)
    pl.semaphore_wait(barrier, n_lon + 1)

    def route_copy(o):
        target = lax.rem(b + o, n_lon)
        return pltpu.make_async_remote_copy(
            src_ref=packed_ref.at[target],
            dst_ref=recv.at[o],
            send_sem=route_send.at[o],
            recv_sem=route_recv.at[o],
            device_id=(a, target),
            device_id_type=MESH,
        )

    def row_copy(step, part, side):
        return pltpu.make_async_remote_copy(
            src_ref=row_out.at[step, side, pl.ds(part * per_part, per_part)],
            dst_ref=row_in.at[step, side, pl.ds(part * per_part, per_part)],
            send_sem=halo_send.at[step, part, side],
            recv_sem=halo_recv.at[step, part, side],
            device_id=(south if side == 0 else north, b),
            device_id_type=MESH,
        )

    def col_copy(step, part, side):
        return pltpu.make_async_remote_copy(
            src_ref=col_out.at[step, side, pl.ds(part * per_part, per_part)],
            dst_ref=col_in.at[step, side, pl.ds(part * per_part, per_part)],
            send_sem=halo_send.at[step, part, 2 + side],
            recv_sem=halo_recv.at[step, part, 2 + side],
            device_id=(a, west if side == 0 else east),
            device_id_type=MESH,
        )

    def send_part(step, part):
        for side in range(2):
            col_copy(step, part, side).start()

        @pl.when(has_south)
        def _():
            row_copy(step, part, 0).start()

        @pl.when(has_north)
        def _():
            row_copy(step, part, 1).start()

    def wait_part(step, part):
        for side in range(2):
            col_copy(step, part, side).wait_recv()

        @pl.when(has_north)
        def _():
            row_copy(step, part, 0).wait_recv()

        @pl.when(has_south)
        def _():
            row_copy(step, part, 1).wait_recv()

    def wait_sent(step, part):
        for side in range(2):
            col_copy(step, part, side).wait_send()

        @pl.when(has_south)
        def _():
            row_copy(step, part, 0).wait_send()

        @pl.when(has_north)
        def _():
            row_copy(step, part, 1).wait_send()

    lanes = lax.broadcasted_iota(jnp.int32, (8, 128), 1)
    subs = lax.broadcasted_iota(jnp.int32, (8, 128), 0)
    zero = jnp.zeros((8, 128), F32)
    first_lane, last_lane = lanes == 0, lanes == 127
    first_sub, last_sub = subs == 0, subs == 7

    def keep_edges(step, block, slot, x, packs):
        row_out[step, 0, block, slot : slot + 1, :] = x[0:1]
        row_out[step, 1, block, slot : slot + 1, :] = x[7:8]
        here = lanes == slot
        return (
            jnp.where(here, jnp.broadcast_to(x[:, 0:1], (8, 128)), packs[0]),
            jnp.where(here, jnp.broadcast_to(x[:, 127:128], (8, 128)), packs[1]),
        )

    def put_packs(step, block, packs):
        col_out[step, 0, block] = packs[0]
        col_out[step, 1, block] = packs[1]

    def over_parts(step, body, carry, wait, send):
        def part_body(part, carry):
            if wait is not None:
                wait_part(wait, part)
            carry = lax.fori_loop(
                part * per_part, (part + 1) * per_part, body, carry
            )
            if send is not None:
                send_part(send, part)
            return carry

        return lax.fori_loop(0, PARTS, part_body, carry)

    def level_at(ascending, block, i):
        count = block * UNROLL + i
        return count if ascending else levels - 1 - count

    for t in range(tracers):
        spot = subs * 128 + lanes
        add = zero
        for s in range(cell_ref.shape[0]):
            add = add + jnp.where(spot == cell_ref[s], misfit_ref[t, s], 0.0)
        field[0, t] = adj_ref[t, 0] + add
    kpad[0] = zero

    def start_body(block, carry):
        packs = (zero, zero)
        for i in range(UNROLL):
            level = block * UNROLL + i
            kpad[level + 1] = k_ref[level]
            for t in range(tracers):
                x = adj_ref[t, level]
                x = jnp.where(level == 0, field[0, t], x)
                field[level, t] = x
                packs = keep_edges(0, block, i * tracers + t, x, packs)
        put_packs(0, block, packs)
        return carry

    over_parts(0, start_body, 0, None, 0)

    def route_start(o, carry):
        route_copy(o).start()
        return carry

    lax.fori_loop(1, n_lon, route_start, 0)

    def factor_body(block, carry):
        for i in range(UNROLL):
            new = []
            for d in range(2):
                level = level_at(d == 0, block, i)
                below, above = kpad[level], kpad[level + 1]
                back, ahead = (below, above) if d == 0 else (above, below)
                inverse = 1.0 / (1.0 + below + above - back * back * carry[d])
                fac[d, 0, level] = inverse
                fac[d, 1, level] = back * inverse
                fac[d, 2, level] = ahead * inverse
                new.append(inverse)
            carry = tuple(new)
        return carry

    lax.fori_loop(0, blocks, factor_body, (zero, zero))

    def advance(step, ascending, emit, send):
        d = 0 if ascending else 1

        def sweep(block, carry):
            ys = list(carry)
            col_e, col_w = col_in[step, 0, block], col_in[step, 1, block]
            for i in range(UNROLL):
                level = level_at(ascending, block, i)
                u, v = u_ref[level], v_ref[level]
                inverse, back = fac[d, 0, level], fac[d, 1, level]
                up, vp = jnp.maximum(u, 0.0), jnp.maximum(v, 0.0)
                un, vn = jnp.maximum(-u, 0.0), jnp.maximum(-v, 0.0)
                own = 1.0 - (up + un) - (vp + vn)
                for t in range(tracers):
                    slot = i * tracers + t
                    c = field[level, t]
                    e = jnp.where(first_lane, pltpu.roll(col_e, (128 - slot) % 128, 1), c)
                    e = pltpu.roll(e, 127, 1)
                    w = jnp.where(last_lane, pltpu.roll(col_w, 127 - slot, 1), c)
                    w = pltpu.roll(w, 1, 1)
                    row_n = jnp.broadcast_to(row_in[step, 0, block, slot : slot + 1, :], (8, 128))
                    row_s = jnp.broadcast_to(row_in[step, 1, block, slot : slot + 1, :], (8, 128))
                    n = jnp.where(last_sub, row_n, pltpu.roll(c, 7, 0))
                    s = jnp.where(first_sub, row_s, pltpu.roll(c, 1, 0))
                    q = (own * c + up * e) + (un * w) + (vp * n + vn * s)
                    y = q * inverse + back * ys[t]
                    y_buf[level, t] = y
                    ys[t] = y
            return tuple(ys)

        over_parts(step, sweep, (zero,) * tracers, step, None)

        def substitute(block, carry):
            xs = list(carry)
            packs = (zero, zero)
            for i in range(UNROLL):
                level = level_at(not ascending, block, i)
                ahead = fac[d, 2, level]
                for t in range(tracers):
                    x = y_buf[level, t] + ahead * xs[t]
                    xs[t] = x
                    emit(level, t, x)
                    if send is not None:
                        packs = keep_edges(send, block, i * tracers + t, x, packs)
            if send is not None:
                put_packs(send, block, packs)
            return tuple(xs)

        over_parts(step, substitute, (zero,) * tracers, None, send)

    def to_field(level, t, x):
        field[level, t] = x

    def to_out(level, t, x):
        out_ref[t, level] = x

    @pl.when(jnp.logical_not(has_north))
    def _():
        for step in range(3):
            row_in[step, 0] = jnp.zeros(row_in.shape[2:], F32)

    @pl.when(jnp.logical_not(has_south))
    def _():
        for step in range(3):
            row_in[step, 1] = jnp.zeros(row_in.shape[2:], F32)

    acc[...] = jnp.zeros_like(acc)
    recv[0] = packed_ref[b]

    advance(0, True, to_field, None)

    def force(o, carry):
        @pl.when(o > 0)
        def _():
            route_copy(o).wait_recv()

        data = jnp.concatenate([recv[o, h] for h in range(chunk)], axis=1)
        height, width = data.shape
        meta = data[height - 16 :].astype(F32)
        lat_row = meta[8 + tracers : 9 + tracers]
        lane = meta[9 + tracers : 10 + tracers].astype(jnp.int32)
        spots = lax.broadcasted_iota(jnp.int32, (128, width), 0)
        hit = jnp.where(spots == lane, 1.0, 0.0).astype(BF16)
        right = jnp.concatenate(
            [hit * meta[8 + t : 9 + t].astype(BF16) for t in range(tracers)], axis=0
        )
        left = jnp.concatenate(
            [data * jnp.where(lat_row == r, 1.0, 0.0).astype(BF16) for r in range(8)], axis=0
        )
        total = lax.dot_general(left, right, NT, preferred_element_type=F32)
        for t in range(tracers):
            acc[t] += total[:, t * 128 : (t + 1) * 128]
        return carry

    lax.fori_loop(0, n_lon, force, 0)

    pitch = acc.shape[1] // 8

    def inject_body(block, carry):
        packs = (zero, zero)
        for i in range(UNROLL):
            level = level_at(False, block, i)
            for t in range(tracers):
                x = field[level, t] + acc[t, pl.ds(level, 8, pitch), :]
                field[level, t] = x
                packs = keep_edges(1, block, i * tracers + t, x, packs)
        put_packs(1, block, packs)
        return carry

    over_parts(1, inject_body, 0, None, 1)
    advance(1, False, to_field, 2)
    advance(2, True, to_out, None)

    def route_sent(o, carry):
        route_copy(o).wait_send()
        return carry

    lax.fori_loop(1, n_lon, route_sent, 0)

    def sent(part, carry):
        for step in range(3):
            wait_sent(step, part)
        return carry

    lax.fori_loop(0, PARTS, sent, 0)


def body(
    n_lat, n_lon,
    adjoint_in, wind_u, wind_v, diffusion, kernel_rows, retrieval_misfit,
    retrieval_columns, retrieval_counts, station_cells, station_misfit,
):
    tracers, levels, lat_rows, lon_cells = adjoint_in.shape
    cols = lat_rows * lon_cells
    slots = kernel_rows.shape[1]
    cap = 2 * slots // n_lon
    width = min(cap, 256)
    chunk = cap // width
    height = levels + 8
    vmem, smem = pl.BlockSpec(memory_space=pltpu.VMEM), pl.BlockSpec(memory_space=pltpu.SMEM)
    packed = pl.pallas_call(
        functools.partial(route_kernel, n_lon, cap, cols, lon_cells),
        out_shape=jax.ShapeDtypeStruct((n_lon * chunk, height, width), BF16),
        in_specs=[smem, vmem, vmem, vmem],
        out_specs=vmem,
        scratch_shapes=[pltpu.VMEM((height, slots), BF16)],
        compiler_params=pltpu.CompilerParams(vmem_limit_bytes=48 * 2**20),
        name="route",
    )(retrieval_counts, kernel_rows, retrieval_misfit, retrieval_columns.reshape(1, slots))
    packed = packed.reshape(n_lon, chunk, height, width)
    blocks = levels // UNROLL
    edge = UNROLL * tracers
    return pl.pallas_call(
        functools.partial(transport_kernel, n_lat, n_lon),
        out_shape=jax.ShapeDtypeStruct(adjoint_in.shape, F32),
        in_specs=[vmem] * 5 + [smem] * 2,
        out_specs=vmem,
        scratch_shapes=[
            pltpu.VMEM((levels, tracers, 8, 128), F32),
            pltpu.VMEM((levels, tracers, 8, 128), F32),
            pltpu.VMEM((levels + 1, 8, 128), F32),
            pltpu.VMEM((2, 3, levels, 8, 128), F32),
            pltpu.VMEM((tracers, 8 * height, 128), F32),
            pltpu.VMEM((n_lon, chunk, height, width), BF16),
            pltpu.VMEM((3, 2, blocks, edge, 128), F32),
            pltpu.VMEM((3, 2, blocks, edge, 128), F32),
            pltpu.VMEM((3, 2, blocks, 8, 128), F32),
            pltpu.VMEM((3, 2, blocks, 8, 128), F32),
            pltpu.SemaphoreType.DMA((n_lon,)),
            pltpu.SemaphoreType.DMA((n_lon,)),
            pltpu.SemaphoreType.DMA((3, PARTS, 4)),
            pltpu.SemaphoreType.DMA((3, PARTS, 4)),
        ],
        compiler_params=pltpu.CompilerParams(
            collective_id=0, has_side_effects=True, vmem_limit_bytes=56 * 2**20
        ),
        name="transport",
    )(adjoint_in, wind_u, wind_v, diffusion, packed, station_cells, station_misfit)


def solution(mesh):
    return jax.shard_map(
        functools.partial(body, mesh.shape["lat"], mesh.shape["lon"]),
        mesh=mesh,
        in_specs=(
            P(None, None, "lat", "lon"),
            P(None, "lat", "lon"),
            P(None, "lat", "lon"),
            P(None, "lat", "lon"),
            P(None, ("lat", "lon")),
            P(None, ("lat", "lon")),
            P(("lat", "lon")),
            P(("lat", "lon")),
            P(("lat", "lon")),
            P(None, ("lat", "lon")),
        ),
        out_specs=P(None, None, "lat", "lon"),
        check_vma=False,
    )
```

```python
import functools

import jax
import jax.numpy as jnp
from jax import lax
from jax.experimental import pallas as pl
from jax.experimental.pallas import tpu as pltpu
from jax.sharding import PartitionSpec as P

MESH = pl.DeviceIdType.MESH
F32 = jnp.float32
BF16 = jnp.bfloat16
UNROLL = 8
PARTS = 3
GROUP = 16
EARLY = 2
NT = (((1,), (1,)), ((), ()))


def transport_kernel(
    n_lat, n_lon,
    adj_hbm, u_hbm, v_hbm, k_hbm, rows_ref, retrieved_ref, column_ref,
    count_ref, cell_ref, misfit_ref,
    out_hbm,
    adj_ref, u_ref, v_ref, out_ref,
    field, y_buf, kpad, fac, acc, pay, packed, recv, weights, spread,
    row_out, row_in, col_out, col_in,
    load_sem, store_sem, route_send, route_recv, halo_send, halo_recv,
):
    tracers, levels = adj_ref.shape[:2]
    slots = rows_ref.shape[1]
    blocks = levels // UNROLL
    a = lax.axis_index("lat")
    b = lax.axis_index("lon")
    north, south = lax.rem(a + 1, n_lat), lax.rem(a + n_lat - 1, n_lat)
    east, west = lax.rem(b + 1, n_lon), lax.rem(b + n_lon - 1, n_lon)
    has_north, has_south = a < n_lat - 1, a > 0
    chunk, height, width = recv.shape[1:]
    cap = chunk * width
    groups = height // GROUP

    loads = [
        pltpu.make_async_copy(adj_hbm, adj_ref, load_sem.at[0]),
        pltpu.make_async_copy(k_hbm, kpad.at[pl.ds(1, levels)], load_sem.at[1]),
        pltpu.make_async_copy(u_hbm, u_ref, load_sem.at[2]),
        pltpu.make_async_copy(v_hbm, v_ref, load_sem.at[3]),
    ]
    for load in loads:
        load.start()

    barrier = pltpu.get_barrier_semaphore()
    for other in (north, south):
        pl.semaphore_signal(barrier, inc=1, device_id=(other, b), device_id_type=MESH)

    def greet(o, carry):
        pl.semaphore_signal(
            barrier, inc=1, device_id=(a, lax.rem(b + o, n_lon)), device_id_type=MESH
        )
        return carry

    lax.fori_loop(1, n_lon, greet, 0)

    def route_copy(o, g):
        target = lax.rem(b + o, n_lon)
        rows = pl.ds(height - (g + 1) * GROUP, GROUP)
        return pltpu.make_async_remote_copy(
            src_ref=packed.at[o, :, rows],
            dst_ref=recv.at[o, :, rows],
            send_sem=route_send.at[o, g],
            recv_sem=route_recv.at[o, g],
            device_id=(a, target),
            device_id_type=MESH,
        )

    def send_group(g):
        def start(o, carry):
            route_copy(o, g).start()
            return carry

        lax.fori_loop(1, n_lon, start, 0)

    def bounds(step):
        if step == 1:
            return [0] + [(g * GROUP + GROUP - 8) // UNROLL for g in range(groups)]
        return [blocks * p // PARTS for p in range(PARTS + 1)]

    def row_copy(step, part, side):
        return pltpu.make_async_remote_copy(
            src_ref=row_out.at[step, side, pl.ds(bounds(step)[part], bounds(step)[part + 1] - bounds(step)[part])],
            dst_ref=row_in.at[step, side, pl.ds(bounds(step)[part], bounds(step)[part + 1] - bounds(step)[part])],
            send_sem=halo_send.at[step, part, side],
            recv_sem=halo_recv.at[step, part, side],
            device_id=(south if side == 0 else north, b),
            device_id_type=MESH,
        )

    def col_copy(step, part, side):
        return pltpu.make_async_remote_copy(
            src_ref=col_out.at[step, side, pl.ds(bounds(step)[part], bounds(step)[part + 1] - bounds(step)[part])],
            dst_ref=col_in.at[step, side, pl.ds(bounds(step)[part], bounds(step)[part + 1] - bounds(step)[part])],
            send_sem=halo_send.at[step, part, 2 + side],
            recv_sem=halo_recv.at[step, part, 2 + side],
            device_id=(a, west if side == 0 else east),
            device_id_type=MESH,
        )

    def send_part(step, part):
        for side in range(2):
            col_copy(step, part, side).start()

        @pl.when(has_south)
        def _():
            row_copy(step, part, 0).start()

        @pl.when(has_north)
        def _():
            row_copy(step, part, 1).start()

    def wait_part(step, part):
        for side in range(2):
            col_copy(step, part, side).wait_recv()

        @pl.when(has_north)
        def _():
            row_copy(step, part, 0).wait_recv()

        @pl.when(has_south)
        def _():
            row_copy(step, part, 1).wait_recv()

    def wait_sent(step, part):
        for side in range(2):
            col_copy(step, part, side).wait_send()

        @pl.when(has_south)
        def _():
            row_copy(step, part, 0).wait_send()

        @pl.when(has_north)
        def _():
            row_copy(step, part, 1).wait_send()

    lanes = lax.broadcasted_iota(jnp.int32, (8, 128), 1)
    subs = lax.broadcasted_iota(jnp.int32, (8, 128), 0)
    zero = jnp.zeros((8, 128), F32)
    first_lane, last_lane = lanes == 0, lanes == 127
    first_sub, last_sub = subs == 0, subs == 7

    def keep_edges(step, block, slot, x, packs):
        row_out[step, 0, block, slot : slot + 1, :] = x[0:1]
        row_out[step, 1, block, slot : slot + 1, :] = x[7:8]
        here = lanes == slot
        return (
            jnp.where(here, jnp.broadcast_to(x[:, 0:1], (8, 128)), packs[0]),
            jnp.where(here, jnp.broadcast_to(x[:, 127:128], (8, 128)), packs[1]),
        )

    def put_packs(step, block, packs):
        col_out[step, 0, block] = packs[0]
        col_out[step, 1, block] = packs[1]

    def over_parts(step, body, carry, wait, send):
        edges = bounds(step)
        for part in range(len(edges) - 1):
            if wait is not None:
                wait_part(wait, part)
            carry = lax.fori_loop(edges[part], edges[part + 1], body, carry)
            if send is not None:
                send_part(send, part)
        return carry

    def level_at(ascending, block, i):
        count = block * UNROLL + i
        return count if ascending else levels - 1 - count

    lat_rows, lon_cells = adj_ref.shape[2:]
    cols = lat_rows * lon_cells
    column = column_ref[...]
    tile = column // cols
    cell = column - tile * cols
    lat_row = cell // lon_cells
    lane = cell - lat_row * lon_cells
    live = lax.broadcasted_iota(jnp.int32, (1, slots), 1) < count_ref[0]
    offset = jnp.where(tile >= b, tile - b, tile - b + n_lon)
    offset = jnp.where(live, offset, -1)
    which = lax.broadcasted_iota(jnp.int32, (n_lon, slots), 0)
    hits = jnp.where(which == offset, 1.0, 0.0).astype(F32)
    step = 256
    before = (
        lax.broadcasted_iota(jnp.int32, (step, step), 0)
        < lax.broadcasted_iota(jnp.int32, (step, step), 1)
    )
    upper = jnp.where(before, 1.0, 0.0).astype(BF16)
    base = jnp.zeros((n_lon, 1), F32)
    ranks = []
    for start in range(0, slots, step):
        part = hits[:, start : start + step]
        ahead = jnp.dot(part.astype(BF16), upper, preferred_element_type=F32) + base
        ranks.append(jnp.sum(part * ahead, axis=0, keepdims=True))
        base = base + jnp.sum(part, axis=1, keepdims=True)
    rank = jnp.concatenate(ranks, axis=1)
    half = jnp.zeros((1, slots), F32)
    for h in range(1, chunk):
        half = half + jnp.where(rank >= float(h * width), 1.0, 0.0)
    place = jnp.where(live, offset.astype(F32) * chunk + half, -1.0)
    within = (rank - half * width).astype(BF16)
    wide = rows_ref[...].astype(F32)
    pay[0 : levels - 8, :] = wide[: levels - 8].astype(BF16)
    tail = jnp.concatenate(
        [
            retrieved_ref[...].astype(F32),
            lat_row.astype(F32),
            lane.astype(F32),
            jnp.zeros((8 - tracers - 2, slots), F32),
        ],
        axis=0,
    )
    pay[levels - 8 : levels + 8, :] = jnp.concatenate([wide[levels - 8 :], tail], axis=0).astype(BF16)
    index = lax.broadcasted_iota(jnp.int32, (width, slots), 0).astype(F32).astype(BF16)
    pick = jnp.where(
        jnp.broadcast_to(within, (width, slots)) == index,
        jnp.ones((width, slots), BF16),
        jnp.zeros((width, slots), BF16),
    )
    weights[...] = pick

    loads[0].wait()
    loads[1].wait()
    for t in range(tracers):
        spot = subs * 128 + lanes
        add = zero
        for s in range(cell_ref.shape[0]):
            add = add + jnp.where(spot == cell_ref[s], misfit_ref[t, s], 0.0)
        adj_ref[t, 0] = adj_ref[t, 0] + add
    kpad[0] = zero

    def start_body(block, carry):
        packs = (zero, zero)
        for i in range(UNROLL):
            level = block * UNROLL + i
            for t in range(tracers):
                packs = keep_edges(0, block, i * tracers + t, adj_ref[t, level], packs)
        put_packs(0, block, packs)
        return carry

    lax.fori_loop(0, blocks, start_body, 0)
    pl.semaphore_wait(barrier, n_lon + 1)
    for part in range(PARTS):
        send_part(0, part)

    several = max(1, 4 // chunk)

    def pack_body(turn, carry):
        picks = []
        for i in range(several * chunk):
            here = (turn * (several * chunk) + i).astype(F32)
            mask = jnp.where(place == here, 1.0, 0.0).astype(BF16)
            picks.append(pay[...] * mask)
        left = jnp.concatenate(picks, axis=0)
        total = lax.dot_general(left, weights[...], NT, preferred_element_type=F32).astype(BF16)
        for i in range(several):
            o = turn * several + i
            for h in range(chunk):
                at = (i * chunk + h) * height
                packed[o, h] = total[at : at + height]

            @pl.when(o > 0)
            def _():
                for g in range(EARLY):
                    route_copy(o, g).start()

        return carry

    lax.fori_loop(0, n_lon // several, pack_body, 0)
    recv[0] = packed[0]
    send_group(EARLY)

    def factor_body(block, carry):
        for i in range(UNROLL):
            new = []
            for d in range(2):
                level = level_at(d == 0, block, i)
                below, above = kpad[level], kpad[level + 1]
                back, ahead = (below, above) if d == 0 else (above, below)
                inverse = 1.0 / (1.0 + below + above - back * back * carry[d])
                fac[d, 0, level] = inverse
                fac[d, 1, level] = back * inverse
                fac[d, 2, level] = ahead * inverse
                new.append(inverse)
            carry = tuple(new)
        return carry

    lax.fori_loop(0, blocks, factor_body, (zero, zero))

    def sweep_of(step, ascending, fetch):
        d = 0 if ascending else 1

        def sweep(block, carry):
            ys = list(carry)
            col_e, col_w = col_in[step, 0, block], col_in[step, 1, block]
            for i in range(UNROLL):
                level = level_at(ascending, block, i)
                u, v = u_ref[level], v_ref[level]
                inverse, back = fac[d, 0, level], fac[d, 1, level]
                up, vp = jnp.maximum(u, 0.0), jnp.maximum(v, 0.0)
                un, vn = jnp.maximum(-u, 0.0), jnp.maximum(-v, 0.0)
                own = 1.0 - (up + un) - (vp + vn)
                for t in range(tracers):
                    slot = i * tracers + t
                    c = fetch(level, t)
                    e = jnp.where(
                        last_lane, pltpu.roll(col_e, 127 - slot, 1), pltpu.roll(c, 127, 1)
                    )
                    w = jnp.where(
                        first_lane, pltpu.roll(col_w, (128 - slot) % 128, 1), pltpu.roll(c, 1, 1)
                    )
                    row_n = jnp.broadcast_to(row_in[step, 0, block, slot : slot + 1, :], (8, 128))
                    row_s = jnp.broadcast_to(row_in[step, 1, block, slot : slot + 1, :], (8, 128))
                    n = jnp.where(last_sub, row_n, pltpu.roll(c, 7, 0))
                    s = jnp.where(first_sub, row_s, pltpu.roll(c, 1, 0))
                    q = (own * c + up * e) + (un * w) + (vp * n + vn * s)
                    y = q * inverse + back * ys[t]
                    y_buf[level, t] = y
                    ys[t] = y
            return tuple(ys)

        return sweep

    def substitute_of(step, ascending, emit, send):
        d = 0 if ascending else 1

        def substitute(block, carry):
            xs = list(carry)
            packs = (zero, zero)
            for i in range(UNROLL):
                level = level_at(not ascending, block, i)
                ahead = fac[d, 2, level]
                for t in range(tracers):
                    x = y_buf[level, t] + ahead * xs[t]
                    xs[t] = x
                    emit(level, t, x)
                    if send is not None:
                        packs = keep_edges(send, block, i * tracers + t, x, packs)
            if send is not None:
                put_packs(send, block, packs)
            return tuple(xs)

        return substitute

    def to_field(level, t, x):
        field[level, t] = x

    def to_out(level, t, x):
        out_ref[t, level] = x

    @pl.when(jnp.logical_not(has_north))
    def _():
        for step in range(3):
            row_in[step, 0] = jnp.zeros(row_in.shape[2:], F32)

    @pl.when(jnp.logical_not(has_south))
    def _():
        for step in range(3):
            row_in[step, 1] = jnp.zeros(row_in.shape[2:], F32)

    def from_field(level, t):
        return field[level, t]

    def from_input(level, t):
        return adj_ref[t, level]

    none = (zero,) * tracers
    loads[2].wait()
    loads[3].wait()
    over_parts(0, sweep_of(0, True, from_input), none, 0, None)
    send_group(EARLY + 1)
    over_parts(0, substitute_of(0, True, to_field, None), none, None, None)

    def read(o, rows):
        return jnp.concatenate([recv[o, h, rows] for h in range(chunk)], axis=1)

    def force(g, o):
        rows = pl.ds(height - (g + 1) * GROUP, GROUP)
        meta = read(o, pl.ds(height - GROUP, GROUP)).astype(F32)
        if g == 0:
            spots = lax.broadcasted_iota(jnp.int32, (128, cap), 0)
            lane_of = meta[GROUP - 7 + tracers : GROUP - 6 + tracers].astype(jnp.int32)
            hit = jnp.where(spots == lane_of, 1.0, 0.0).astype(BF16)
            for t in range(tracers):
                misfit = meta[GROUP - 8 + t : GROUP - 7 + t].astype(BF16)
                spread[o, t * 128 : (t + 1) * 128] = hit * misfit
        row_of = meta[GROUP - 8 + tracers : GROUP - 7 + tracers]
        data = read(o, rows)
        left = jnp.concatenate(
            [data * jnp.where(row_of == r, 1.0, 0.0).astype(BF16) for r in range(8)], axis=0
        )
        return lax.dot_general(left, spread[o], NT, preferred_element_type=F32)

    sweep_1 = sweep_of(1, False, from_field)
    edges = bounds(1)
    ys = none
    for g in range(groups):
        first = force(g, 0)
        for t in range(tracers):
            acc[t] = first[:, t * 128 : (t + 1) * 128]

        def force_body(o, carry, g=g):
            route_copy(o, g).wait_recv()
            total = force(g, o)
            for t in range(tracers):
                acc[t] += total[:, t * 128 : (t + 1) * 128]
            return carry

        lax.fori_loop(1, n_lon, force_body, 0)
        if EARLY + 2 + g < groups:
            send_group(EARLY + 2 + g)

        def inject_body(block, carry, g=g):
            packs = (zero, zero)
            for i in range(UNROLL):
                level = level_at(False, block, i)
                row = level - (levels + 8 - (g + 1) * GROUP)
                for t in range(tracers):
                    x = field[level, t] + acc[t, pl.ds(row, 8, GROUP), :]
                    field[level, t] = x
                    packs = keep_edges(1, block, i * tracers + t, x, packs)
            put_packs(1, block, packs)
            return carry

        lax.fori_loop(edges[g], edges[g + 1], inject_body, 0)
        send_part(1, g)
        if g > 0:
            wait_part(1, g - 1)
            ys = lax.fori_loop(edges[g - 1], edges[g], sweep_1, ys)
    wait_part(1, groups - 1)
    lax.fori_loop(edges[groups - 1], edges[groups], sweep_1, ys)
    over_parts(0, substitute_of(1, False, to_field, 2), none, None, 2)

    over_parts(2, sweep_of(2, True, from_field), none, 2, None)
    last = substitute_of(2, True, to_out, None)
    edges = bounds(2)
    stores = []
    carry = none
    for part in range(PARTS):
        carry = lax.fori_loop(edges[part], edges[part + 1], last, carry)
        some = pl.ds(levels - edges[part + 1] * UNROLL, (edges[part + 1] - edges[part]) * UNROLL)
        store = pltpu.make_async_copy(
            out_ref.at[:, some], out_hbm.at[:, some], store_sem.at[part]
        )
        store.start()
        stores.append(store)

    def route_sent(o, carry):
        for g in range(groups):
            route_copy(o, g).wait_send()
        return carry

    lax.fori_loop(1, n_lon, route_sent, 0)
    for step in range(3):
        for part in range(len(bounds(step)) - 1):
            wait_sent(step, part)
    for store in stores:
        store.wait()


def body(
    n_lat, n_lon,
    adjoint_in, wind_u, wind_v, diffusion, kernel_rows, retrieval_misfit,
    retrieval_columns, retrieval_counts, station_cells, station_misfit,
):
    tracers, levels, lat_rows, lon_cells = adjoint_in.shape
    cols = lat_rows * lon_cells
    slots = kernel_rows.shape[1]
    cap = 2 * slots // n_lon
    width = min(cap, 256)
    chunk = cap // width
    height = levels + 8
    any_space = pl.BlockSpec(memory_space=pl.ANY)
    vmem, smem = pl.BlockSpec(memory_space=pltpu.VMEM), pl.BlockSpec(memory_space=pltpu.SMEM)
    groups = height // GROUP
    blocks = levels // UNROLL
    edge = UNROLL * tracers
    return pl.pallas_call(
        functools.partial(transport_kernel, n_lat, n_lon),
        out_shape=jax.ShapeDtypeStruct(adjoint_in.shape, F32),
        in_specs=[any_space] * 4 + [vmem] * 3 + [smem] * 3,
        out_specs=any_space,
        scratch_shapes=[
            pltpu.VMEM(adjoint_in.shape, F32),
            pltpu.VMEM(wind_u.shape, F32),
            pltpu.VMEM(wind_v.shape, F32),
            pltpu.VMEM(adjoint_in.shape, F32),
            pltpu.VMEM((levels, tracers, 8, 128), F32),
            pltpu.VMEM((levels, tracers, 8, 128), F32),
            pltpu.VMEM((levels + 1, 8, 128), F32),
            pltpu.VMEM((2, 3, levels, 8, 128), F32),
            pltpu.VMEM((tracers, 8 * GROUP, 128), F32),
            pltpu.VMEM((height, slots), BF16),
            pltpu.VMEM((n_lon, chunk, height, width), BF16),
            pltpu.VMEM((n_lon, chunk, height, width), BF16),
            pltpu.VMEM((width, slots), BF16),
            pltpu.VMEM((n_lon, tracers * 128, cap), BF16),
            pltpu.VMEM((3, 2, blocks, edge, 128), F32),
            pltpu.VMEM((3, 2, blocks, edge, 128), F32),
            pltpu.VMEM((3, 2, blocks, 8, 128), F32),
            pltpu.VMEM((3, 2, blocks, 8, 128), F32),
            pltpu.SemaphoreType.DMA((4,)),
            pltpu.SemaphoreType.DMA((PARTS,)),
            pltpu.SemaphoreType.DMA((n_lon, groups)),
            pltpu.SemaphoreType.DMA((n_lon, groups)),
            pltpu.SemaphoreType.DMA((3, max(groups, PARTS), 4)),
            pltpu.SemaphoreType.DMA((3, max(groups, PARTS), 4)),
        ],
        compiler_params=pltpu.CompilerParams(
            collective_id=0, has_side_effects=True, vmem_limit_bytes=40 * 2**20
        ),
        name="transport",
    )(
        adjoint_in, wind_u, wind_v, diffusion, kernel_rows, retrieval_misfit,
        retrieval_columns.reshape(1, slots), retrieval_counts, station_cells, station_misfit,
    )


def solution(mesh):
    return jax.shard_map(
        functools.partial(body, mesh.shape["lat"], mesh.shape["lon"]),
        mesh=mesh,
        in_specs=(
            P(None, None, "lat", "lon"),
            P(None, "lat", "lon"),
            P(None, "lat", "lon"),
            P(None, "lat", "lon"),
            P(None, ("lat", "lon")),
            P(None, ("lat", "lon")),
            P(("lat", "lon")),
            P(("lat", "lon")),
            P(("lat", "lon")),
            P(None, ("lat", "lon")),
        ),
        out_specs=P(None, None, "lat", "lon"),
        check_vma=False,
    )
```

```python
import functools

import jax
import jax.numpy as jnp
from jax import lax
from jax.experimental import pallas as pl
from jax.experimental.pallas import tpu as pltpu
from jax.sharding import PartitionSpec as P

MESH = pl.DeviceIdType.MESH
F32 = jnp.float32
BF16 = jnp.bfloat16
UNROLL = 8
PARTS = 3
GROUP = 16
EARLY = 2
NT = (((1,), (1,)), ((), ()))


def transport_kernel(
    n_lat, n_lon,
    adj_hbm, u_hbm, v_hbm, k_hbm, rows_hbm, retrieved_hbm, column_hbm,
    count_ref, cell_hbm, misfit_hbm,
    out_hbm,
    adj_ref, u_ref, v_ref, rows_ref, retrieved_ref, column_ref, cell_ref, misfit_ref, out_ref,
    field, y_buf, kpad, fac, acc, pay, packed, recv, weights, spread, masks, left,
    row_out, row_in, col_out, col_in,
    load_sem, store_sem, route_send, route_recv, halo_send, halo_recv,
):
    tracers, levels = adj_ref.shape[:2]
    slots = rows_ref.shape[1]
    blocks = levels // UNROLL
    a = lax.axis_index("lat")
    b = lax.axis_index("lon")
    north, south = lax.rem(a + 1, n_lat), lax.rem(a + n_lat - 1, n_lat)
    east, west = lax.rem(b + 1, n_lon), lax.rem(b + n_lon - 1, n_lon)
    has_north, has_south = a < n_lat - 1, a > 0
    height, cap = packed.shape[1:]
    width = weights.shape[0]
    chunk = cap // width
    groups = height // GROUP

    loads = [
        pltpu.make_async_copy(adj_hbm, adj_ref, load_sem.at[0]),
        pltpu.make_async_copy(k_hbm, kpad.at[pl.ds(1, levels)], load_sem.at[1]),
        pltpu.make_async_copy(u_hbm, u_ref, load_sem.at[2]),
        pltpu.make_async_copy(v_hbm, v_ref, load_sem.at[3]),
        pltpu.make_async_copy(rows_hbm, rows_ref, load_sem.at[4]),
        pltpu.make_async_copy(retrieved_hbm, retrieved_ref, load_sem.at[5]),
        pltpu.make_async_copy(column_hbm, column_ref, load_sem.at[6]),
        pltpu.make_async_copy(cell_hbm, cell_ref, load_sem.at[7]),
        pltpu.make_async_copy(misfit_hbm, misfit_ref, load_sem.at[8]),
    ]
    for load in loads:
        load.start()

    barrier = pltpu.get_barrier_semaphore()
    for other in (north, south):
        pl.semaphore_signal(barrier, inc=1, device_id=(other, b), device_id_type=MESH)

    def greet(o, carry):
        pl.semaphore_signal(
            barrier, inc=1, device_id=(a, lax.rem(b + o, n_lon)), device_id_type=MESH
        )
        return carry

    lax.fori_loop(1, n_lon, greet, 0)

    def group_rows(g):
        return pl.ds(pl.multiple_of(height - (g + 1) * GROUP, GROUP), GROUP)

    def route_copy(o, g):
        target = lax.rem(b + o, n_lon)
        rows = group_rows(g)
        return pltpu.make_async_remote_copy(
            src_ref=packed.at[o, rows],
            dst_ref=recv.at[rows, pl.ds(pl.multiple_of(o * cap, 128), cap)],
            send_sem=route_send.at[o, g],
            recv_sem=route_recv.at[o, g],
            device_id=(a, target),
            device_id_type=MESH,
        )

    def send_group(g):
        def start(o, carry):
            route_copy(o, g).start()
            return carry

        lax.fori_loop(1, n_lon, start, 0)

    def part_size(step):
        return GROUP // UNROLL if step == 1 else blocks // PARTS

    def place_of(step, block):
        return block + 1 if step == 1 else block

    def row_copy(step, part, side):
        return pltpu.make_async_remote_copy(
            src_ref=row_out.at[step, side, pl.ds(part * part_size(step), part_size(step))],
            dst_ref=row_in.at[step, side, pl.ds(part * part_size(step), part_size(step))],
            send_sem=halo_send.at[step, part, side],
            recv_sem=halo_recv.at[step, part, side],
            device_id=(south if side == 0 else north, b),
            device_id_type=MESH,
        )

    def col_copy(step, part, side):
        return pltpu.make_async_remote_copy(
            src_ref=col_out.at[step, side, pl.ds(part * part_size(step), part_size(step))],
            dst_ref=col_in.at[step, side, pl.ds(part * part_size(step), part_size(step))],
            send_sem=halo_send.at[step, part, 2 + side],
            recv_sem=halo_recv.at[step, part, 2 + side],
            device_id=(a, west if side == 0 else east),
            device_id_type=MESH,
        )

    def send_part(step, part):
        for side in range(2):
            col_copy(step, part, side).start()

        @pl.when(has_south)
        def _():
            row_copy(step, part, 0).start()

        @pl.when(has_north)
        def _():
            row_copy(step, part, 1).start()

    def wait_part(step, part):
        for side in range(2):
            col_copy(step, part, side).wait_recv()

        @pl.when(has_north)
        def _():
            row_copy(step, part, 0).wait_recv()

        @pl.when(has_south)
        def _():
            row_copy(step, part, 1).wait_recv()

    def wait_sent(step, part):
        for side in range(2):
            col_copy(step, part, side).wait_send()

        @pl.when(has_south)
        def _():
            row_copy(step, part, 0).wait_send()

        @pl.when(has_north)
        def _():
            row_copy(step, part, 1).wait_send()

    lanes = lax.broadcasted_iota(jnp.int32, (8, 128), 1)
    subs = lax.broadcasted_iota(jnp.int32, (8, 128), 0)
    zero = jnp.zeros((8, 128), F32)
    first_lane, last_lane = lanes == 0, lanes == 127
    first_sub, last_sub = subs == 0, subs == 7

    def keep_edges(step, block, slot, x, packs):
        row_out[step, 0, place_of(step, block), slot : slot + 1, :] = x[0:1]
        row_out[step, 1, place_of(step, block), slot : slot + 1, :] = x[7:8]
        here = lanes == slot
        return (
            jnp.where(here, jnp.broadcast_to(x[:, 0:1], (8, 128)), packs[0]),
            jnp.where(here, jnp.broadcast_to(x[:, 127:128], (8, 128)), packs[1]),
        )

    def put_packs(step, block, packs):
        col_out[step, 0, place_of(step, block)] = packs[0]
        col_out[step, 1, place_of(step, block)] = packs[1]

    def over_parts(step, body, carry, wait, send):
        size = part_size(step)

        def part_body(part, carry):
            if wait is not None:
                wait_part(wait, part)
            carry = lax.fori_loop(part * size, (part + 1) * size, body, carry)
            if send is not None:
                send_part(send, part)
            return carry

        return lax.fori_loop(0, blocks // size, part_body, carry)

    def level_at(ascending, block, i):
        count = block * UNROLL + i
        return count if ascending else levels - 1 - count

    lat_rows, lon_cells = adj_ref.shape[2:]
    cols = lat_rows * lon_cells
    loads[6].wait()
    column = column_ref[...]
    tile = column // cols
    cell = column - tile * cols
    lat_row = cell // lon_cells
    lane = cell - lat_row * lon_cells
    live = lax.broadcasted_iota(jnp.int32, (1, slots), 1) < count_ref[0]
    offset = jnp.where(tile >= b, tile - b, tile - b + n_lon)
    offset = jnp.where(live, offset, -1)
    which = lax.broadcasted_iota(jnp.int32, (n_lon, slots), 0)
    hits = jnp.where(which == offset, 1.0, 0.0).astype(F32)
    step = 256
    before = (
        lax.broadcasted_iota(jnp.int32, (step, step), 0)
        < lax.broadcasted_iota(jnp.int32, (step, step), 1)
    )
    upper = jnp.where(before, 1.0, 0.0).astype(BF16)
    base = jnp.zeros((n_lon, 1), F32)
    ranks = []
    for start in range(0, slots, step):
        part = hits[:, start : start + step]
        ahead = jnp.dot(part.astype(BF16), upper, preferred_element_type=F32) + base
        ranks.append(jnp.sum(part * ahead, axis=0, keepdims=True))
        base = base + jnp.sum(part, axis=1, keepdims=True)
    rank = jnp.concatenate(ranks, axis=1)
    half = jnp.zeros((1, slots), F32)
    for h in range(1, chunk):
        half = half + jnp.where(rank >= float(h * width), 1.0, 0.0)
    place = jnp.where(live, offset.astype(F32) * chunk + half, -1.0)
    within = (rank - half * width).astype(BF16)
    loads[4].wait()
    loads[5].wait()
    wide = rows_ref[...].astype(F32)
    pay[0 : levels - 8, :] = wide[: levels - 8].astype(BF16)
    tail = jnp.concatenate(
        [
            retrieved_ref[...].astype(F32),
            lat_row.astype(F32),
            lane.astype(F32),
            jnp.zeros((8 - tracers - 2, slots), F32),
        ],
        axis=0,
    )
    pay[levels - 8 : levels + 8, :] = jnp.concatenate([wide[levels - 8 :], tail], axis=0).astype(BF16)
    index = lax.broadcasted_iota(jnp.int32, (width, slots), 0).astype(F32).astype(BF16)
    pick = jnp.where(
        jnp.broadcast_to(within, (width, slots)) == index,
        jnp.ones((width, slots), BF16),
        jnp.zeros((width, slots), BF16),
    )
    weights[...] = pick

    for n in (0, 1, 7, 8):
        loads[n].wait()
    station_cell, station_misfit = cell_ref[...], misfit_ref[...]
    for t in range(tracers):
        spot = subs * 128 + lanes
        add = zero
        for s in range(cell_ref.shape[1]):
            at = jnp.broadcast_to(station_cell[:, s : s + 1], (8, 128))
            term = jnp.broadcast_to(station_misfit[t : t + 1, s : s + 1], (8, 128))
            add = add + jnp.where(spot == at, term, 0.0)
        adj_ref[t, 0] = adj_ref[t, 0] + add
    kpad[0] = zero

    def start_body(block, carry):
        packs = (zero, zero)
        for i in range(UNROLL):
            level = block * UNROLL + i
            for t in range(tracers):
                packs = keep_edges(0, block, i * tracers + t, adj_ref[t, level], packs)
        put_packs(0, block, packs)
        return carry

    lax.fori_loop(0, blocks, start_body, 0)
    pl.semaphore_wait(barrier, n_lon + 1)
    for side in range(2):
        row_out[1, side, 0] = jnp.zeros(row_out.shape[3:], F32)
        col_out[1, side, 0] = zero

    def send_first(part, carry):
        send_part(0, part)
        return carry

    lax.fori_loop(0, PARTS, send_first, 0)

    several = max(1, 4 // chunk)

    def pack_body(turn, carry):
        picks = []
        for i in range(several * chunk):
            here = (turn * (several * chunk) + i).astype(F32)
            mask = jnp.where(place == here, 1.0, 0.0).astype(BF16)
            picks.append(pay[...] * mask)
        stacked = jnp.concatenate(picks, axis=0)
        total = lax.dot_general(stacked, weights[...], NT, preferred_element_type=F32).astype(BF16)
        for i in range(several):
            o = turn * several + i
            for h in range(chunk):
                at = (i * chunk + h) * height
                packed[o, :, h * width : (h + 1) * width] = total[at : at + height]

            @pl.when(o > 0)
            def _():
                for g in range(EARLY):
                    route_copy(o, g).start()

        return carry

    lax.fori_loop(0, n_lon // several, pack_body, 0)
    recv[:, 0:cap] = packed[0]
    send_group(EARLY)

    def factor_body(block, carry):
        for i in range(UNROLL):
            new = []
            for d in range(2):
                level = level_at(d == 0, block, i)
                below, above = kpad[level], kpad[level + 1]
                back, ahead = (below, above) if d == 0 else (above, below)
                inverse = 1.0 / (1.0 + below + above - back * back * carry[d])
                fac[d, 0, level] = inverse
                fac[d, 1, level] = back * inverse
                fac[d, 2, level] = ahead * inverse
                new.append(inverse)
            carry = tuple(new)
        return carry

    lax.fori_loop(0, blocks, factor_body, (zero, zero))

    def sweep_of(step, ascending, fetch):
        d = 0 if ascending else 1

        def sweep(block, carry):
            ys = list(carry)
            spot = place_of(step, block)
            col_e, col_w = col_in[step, 0, spot], col_in[step, 1, spot]
            for i in range(UNROLL):
                level = level_at(ascending, block, i)
                u, v = u_ref[level], v_ref[level]
                inverse, back = fac[d, 0, level], fac[d, 1, level]
                up, vp = jnp.maximum(u, 0.0), jnp.maximum(v, 0.0)
                un, vn = jnp.maximum(-u, 0.0), jnp.maximum(-v, 0.0)
                own = 1.0 - (up + un) - (vp + vn)
                for t in range(tracers):
                    slot = i * tracers + t
                    c = fetch(level, t)
                    e = jnp.where(
                        last_lane, pltpu.roll(col_e, 127 - slot, 1), pltpu.roll(c, 127, 1)
                    )
                    w = jnp.where(
                        first_lane, pltpu.roll(col_w, (128 - slot) % 128, 1), pltpu.roll(c, 1, 1)
                    )
                    row_n = jnp.broadcast_to(row_in[step, 0, spot, slot : slot + 1, :], (8, 128))
                    row_s = jnp.broadcast_to(row_in[step, 1, spot, slot : slot + 1, :], (8, 128))
                    n = jnp.where(last_sub, row_n, pltpu.roll(c, 7, 0))
                    s = jnp.where(first_sub, row_s, pltpu.roll(c, 1, 0))
                    q = (own * c + up * e) + (un * w) + (vp * n + vn * s)
                    y = q * inverse + back * ys[t]
                    y_buf[level, t] = y
                    ys[t] = y
            return tuple(ys)

        return sweep

    def substitute_of(step, ascending, emit, send):
        d = 0 if ascending else 1

        def substitute(block, carry):
            xs = list(carry)
            packs = (zero, zero)
            for i in range(UNROLL):
                level = level_at(not ascending, block, i)
                ahead = fac[d, 2, level]
                for t in range(tracers):
                    x = y_buf[level, t] + ahead * xs[t]
                    xs[t] = x
                    emit(level, t, x)
                    if send is not None:
                        packs = keep_edges(send, block, i * tracers + t, x, packs)
            if send is not None:
                put_packs(send, block, packs)
            return tuple(xs)

        return substitute

    def to_field(level, t, x):
        field[level, t] = x

    def to_out(level, t, x):
        out_ref[t, level] = x

    @pl.when(jnp.logical_not(has_north))
    def _():
        for step in range(3):
            row_in[step, 0] = jnp.zeros(row_in.shape[2:], F32)

    @pl.when(jnp.logical_not(has_south))
    def _():
        for step in range(3):
            row_in[step, 1] = jnp.zeros(row_in.shape[2:], F32)

    def from_field(level, t):
        return field[level, t]

    def from_input(level, t):
        return adj_ref[t, level]

    none = (zero,) * tracers
    loads[2].wait()
    loads[3].wait()
    over_parts(0, sweep_of(0, True, from_input), none, 0, None)
    send_group(EARLY + 1)
    over_parts(0, substitute_of(0, True, to_field, None), none, None, None)

    total_slots = n_lon * cap
    piece = min(512, total_slots)

    def prepare(n, carry):
        here = pl.ds(pl.multiple_of(n * piece, 128), piece)
        meta = recv[height - GROUP : height, here].astype(F32)
        spots = lax.broadcasted_iota(jnp.int32, (128, piece), 0)
        lane_of = meta[GROUP - 7 + tracers : GROUP - 6 + tracers].astype(jnp.int32)
        hit = jnp.where(spots == lane_of, 1.0, 0.0).astype(BF16)
        for t in range(tracers):
            misfit = meta[GROUP - 8 + t : GROUP - 7 + t].astype(BF16)
            spread[t * 128 : (t + 1) * 128, here] = hit * misfit
        row_of = meta[GROUP - 8 + tracers : GROUP - 7 + tracers]
        for r in range(8):
            mask = jnp.where(row_of == r, 1.0, 0.0).astype(BF16)
            masks[r, :, here] = jnp.broadcast_to(mask, (GROUP, piece))
        return carry

    sweep_1 = sweep_of(1, False, from_field)

    def group_edge(g):
        return jnp.maximum(g * (GROUP // UNROLL) - 1, 0)

    def group_body(g, ys):
        def arrived(o, carry):
            route_copy(o, g).wait_recv()
            return carry

        lax.fori_loop(1, n_lon, arrived, 0)

        @pl.when(g + EARLY + 2 < groups)
        def _():
            send_group(g + EARLY + 2)

        @pl.when(g == 0)
        def _():
            lax.fori_loop(0, total_slots // piece, prepare, 0)

        data = recv[group_rows(g), :]
        for r in range(8):
            left[r * GROUP : (r + 1) * GROUP, :] = data * masks[r]
        acc_all = lax.dot_general(left[...], spread[...], NT, preferred_element_type=F32)
        for t in range(tracers):
            acc[t] = acc_all[:, t * 128 : (t + 1) * 128]

        def inject_body(block, carry):
            packs = (zero, zero)
            for i in range(UNROLL):
                level = level_at(False, block, i)
                row = level - (levels + 8 - (g + 1) * GROUP)
                for t in range(tracers):
                    x = field[level, t] + acc[t, pl.ds(row, 8, GROUP), :]
                    field[level, t] = x
                    packs = keep_edges(1, block, i * tracers + t, x, packs)
            put_packs(1, block, packs)
            return carry

        lax.fori_loop(group_edge(g), group_edge(g + 1), inject_body, 0)
        send_part(1, g)

        @pl.when(g > 0)
        def _():
            wait_part(1, g - 1)

        return lax.fori_loop(group_edge(g - 1), group_edge(g), sweep_1, ys)

    ys = lax.fori_loop(0, groups, group_body, none)
    wait_part(1, groups - 1)
    lax.fori_loop(group_edge(groups - 1), group_edge(groups), sweep_1, ys)
    over_parts(0, substitute_of(1, False, to_field, 2), none, None, 2)

    over_parts(2, sweep_of(2, True, from_field), none, 2, None)
    last = substitute_of(2, True, to_out, None)
    size = part_size(2)

    def store(part):
        some = pl.ds(levels - (part + 1) * size * UNROLL, size * UNROLL)
        return pltpu.make_async_copy(out_ref.at[:, some], out_hbm.at[:, some], store_sem.at[part])

    def final(part, carry):
        carry = lax.fori_loop(part * size, (part + 1) * size, last, carry)
        store(part).start()
        return carry

    lax.fori_loop(0, PARTS, final, none)

    def route_sent(o, carry):
        for g in range(groups):
            route_copy(o, g).wait_send()
        return carry

    lax.fori_loop(1, n_lon, route_sent, 0)
    for step in range(3):

        def sent(part, carry, step=step):
            wait_sent(step, part)
            return carry

        lax.fori_loop(0, groups if step == 1 else PARTS, sent, 0)

    def stored(part, carry):
        store(part).wait()
        return carry

    lax.fori_loop(0, PARTS, stored, 0)


def body(
    n_lat, n_lon,
    adjoint_in, wind_u, wind_v, diffusion, kernel_rows, retrieval_misfit,
    retrieval_columns, retrieval_counts, station_cells, station_misfit,
):
    tracers, levels, lat_rows, lon_cells = adjoint_in.shape
    cols = lat_rows * lon_cells
    slots = kernel_rows.shape[1]
    cap = 2 * slots // n_lon
    width = min(cap, 256)
    height = levels + 8
    any_space = pl.BlockSpec(memory_space=pl.ANY)
    hbm = pl.BlockSpec(memory_space=pltpu.HBM)
    stations = station_cells.shape[0]
    smem = pl.BlockSpec(memory_space=pltpu.SMEM)
    groups = height // GROUP
    blocks = levels // UNROLL
    edge = UNROLL * tracers
    return pl.pallas_call(
        functools.partial(transport_kernel, n_lat, n_lon),
        out_shape=jax.ShapeDtypeStruct(adjoint_in.shape, F32),
        in_specs=[hbm] * 7 + [smem] + [hbm] * 2,
        out_specs=any_space,
        scratch_shapes=[
            pltpu.VMEM(adjoint_in.shape, F32),
            pltpu.VMEM(wind_u.shape, F32),
            pltpu.VMEM(wind_v.shape, F32),
            pltpu.VMEM(kernel_rows.shape, BF16),
            pltpu.VMEM(retrieval_misfit.shape, BF16),
            pltpu.VMEM((1, slots), jnp.int32),
            pltpu.VMEM((1, stations), jnp.int32),
            pltpu.VMEM(station_misfit.shape, F32),
            pltpu.VMEM(adjoint_in.shape, F32),
            pltpu.VMEM((levels, tracers, 8, 128), F32),
            pltpu.VMEM((levels, tracers, 8, 128), F32),
            pltpu.VMEM((levels + 1, 8, 128), F32),
            pltpu.VMEM((2, 3, levels, 8, 128), F32),
            pltpu.VMEM((tracers, 8 * GROUP, 128), F32),
            pltpu.VMEM((height, slots), BF16),
            pltpu.VMEM((n_lon, height, cap), BF16),
            pltpu.VMEM((height, n_lon * cap), BF16),
            pltpu.VMEM((width, slots), BF16),
            pltpu.VMEM((tracers * 128, n_lon * cap), BF16),
            pltpu.VMEM((8, GROUP, n_lon * cap), BF16),
            pltpu.VMEM((8 * GROUP, n_lon * cap), BF16),
            pltpu.VMEM((3, 2, blocks + 1, edge, 128), F32),
            pltpu.VMEM((3, 2, blocks + 1, edge, 128), F32),
            pltpu.VMEM((3, 2, blocks + 1, 8, 128), F32),
            pltpu.VMEM((3, 2, blocks + 1, 8, 128), F32),
            pltpu.SemaphoreType.DMA((9,)),
            pltpu.SemaphoreType.DMA((PARTS,)),
            pltpu.SemaphoreType.DMA((n_lon, groups)),
            pltpu.SemaphoreType.DMA((n_lon, groups)),
            pltpu.SemaphoreType.DMA((3, max(groups, PARTS), 4)),
            pltpu.SemaphoreType.DMA((3, max(groups, PARTS), 4)),
        ],
        compiler_params=pltpu.CompilerParams(
            collective_id=0, has_side_effects=True, vmem_limit_bytes=40 * 2**20
        ),
        name="transport",
    )(
        adjoint_in, wind_u, wind_v, diffusion, kernel_rows, retrieval_misfit,
        retrieval_columns.reshape(1, slots), retrieval_counts, station_cells.reshape(1, stations), station_misfit,
    )


def solution(mesh):
    return jax.shard_map(
        functools.partial(body, mesh.shape["lat"], mesh.shape["lon"]),
        mesh=mesh,
        in_specs=(
            P(None, None, "lat", "lon"),
            P(None, "lat", "lon"),
            P(None, "lat", "lon"),
            P(None, "lat", "lon"),
            P(None, ("lat", "lon")),
            P(None, ("lat", "lon")),
            P(("lat", "lon")),
            P(("lat", "lon")),
            P(("lat", "lon")),
            P(None, ("lat", "lon")),
        ),
        out_specs=P(None, None, "lat", "lon"),
        check_vma=False,
    )
```

```python
import functools

import jax
import jax.numpy as jnp
from jax import lax
from jax.experimental import pallas as pl
from jax.experimental.pallas import tpu as pltpu
from jax.sharding import PartitionSpec as P

MESH = pl.DeviceIdType.MESH
F32 = jnp.float32
BF16 = jnp.bfloat16
UNROLL = 8
PARTS = 3
GROUP = 16
EARLY = 2
TN = (((0,), (0,)), ((), ()))


def transport_kernel(
    n_lat, n_lon,
    adj_hbm, u_hbm, v_hbm, k_hbm, rows_hbm, retrieved_hbm, column_hbm,
    count_ref, cell_hbm, misfit_hbm,
    out_hbm,
    adj_ref, u_ref, v_ref, rows_ref, retrieved_ref, column_ref, cell_ref, misfit_ref, out_ref,
    field, y_buf, kpad, fac, acc, pay, packed, recv, weights, spread, masks, left,
    row_out, row_in, col_out, col_in,
    load_sem, store_sem, route_send, route_recv, halo_send, halo_recv,
):
    tracers, levels = adj_ref.shape[:2]
    slots = rows_ref.shape[1]
    blocks = levels // UNROLL
    a = lax.axis_index("lat")
    b = lax.axis_index("lon")
    north, south = lax.rem(a + 1, n_lat), lax.rem(a + n_lat - 1, n_lat)
    east, west = lax.rem(b + 1, n_lon), lax.rem(b + n_lon - 1, n_lon)
    has_north, has_south = a < n_lat - 1, a > 0
    height, cap = packed.shape[1:]
    width = weights.shape[1]
    chunk = cap // width
    groups = height // GROUP

    loads = [
        pltpu.make_async_copy(adj_hbm, adj_ref, load_sem.at[0]),
        pltpu.make_async_copy(k_hbm, kpad.at[pl.ds(1, levels)], load_sem.at[1]),
        pltpu.make_async_copy(u_hbm, u_ref, load_sem.at[2]),
        pltpu.make_async_copy(v_hbm, v_ref, load_sem.at[3]),
        pltpu.make_async_copy(rows_hbm, rows_ref, load_sem.at[4]),
        pltpu.make_async_copy(retrieved_hbm, retrieved_ref, load_sem.at[5]),
        pltpu.make_async_copy(column_hbm, column_ref, load_sem.at[6]),
        pltpu.make_async_copy(cell_hbm, cell_ref, load_sem.at[7]),
        pltpu.make_async_copy(misfit_hbm, misfit_ref, load_sem.at[8]),
    ]
    for load in loads:
        load.start()

    barrier = pltpu.get_barrier_semaphore()
    for other in (north, south):
        pl.semaphore_signal(barrier, inc=1, device_id=(other, b), device_id_type=MESH)

    def greet(o, carry):
        pl.semaphore_signal(
            barrier, inc=1, device_id=(a, lax.rem(b + o, n_lon)), device_id_type=MESH
        )
        return carry

    lax.fori_loop(1, n_lon, greet, 0)

    def group_rows(g):
        return pl.ds(pl.multiple_of(height - (g + 1) * GROUP, GROUP), GROUP)

    def route_copy(o, g):
        target = lax.rem(b + o, n_lon)
        rows = group_rows(g)
        return pltpu.make_async_remote_copy(
            src_ref=packed.at[o, rows],
            dst_ref=recv.at[rows, pl.ds(pl.multiple_of(o * cap, 128), cap)],
            send_sem=route_send.at[o, g],
            recv_sem=route_recv.at[o, g],
            device_id=(a, target),
            device_id_type=MESH,
        )

    def send_group(g):
        def start(o, carry):
            route_copy(o, g).start()
            return carry

        lax.fori_loop(1, n_lon, start, 0)

    def part_size(step):
        return GROUP // UNROLL if step == 1 else blocks // PARTS

    def place_of(step, block):
        return block + 1 if step == 1 else block

    def row_copy(step, part, side):
        return pltpu.make_async_remote_copy(
            src_ref=row_out.at[step, side, pl.ds(part * part_size(step), part_size(step))],
            dst_ref=row_in.at[step, side, pl.ds(part * part_size(step), part_size(step))],
            send_sem=halo_send.at[step, part, side],
            recv_sem=halo_recv.at[step, part, side],
            device_id=(south if side == 0 else north, b),
            device_id_type=MESH,
        )

    def col_copy(step, part, side):
        return pltpu.make_async_remote_copy(
            src_ref=col_out.at[step, side, pl.ds(part * part_size(step), part_size(step))],
            dst_ref=col_in.at[step, side, pl.ds(part * part_size(step), part_size(step))],
            send_sem=halo_send.at[step, part, 2 + side],
            recv_sem=halo_recv.at[step, part, 2 + side],
            device_id=(a, west if side == 0 else east),
            device_id_type=MESH,
        )

    def send_part(step, part):
        for side in range(2):
            col_copy(step, part, side).start()

        @pl.when(has_south)
        def _():
            row_copy(step, part, 0).start()

        @pl.when(has_north)
        def _():
            row_copy(step, part, 1).start()

    def wait_part(step, part):
        for side in range(2):
            col_copy(step, part, side).wait_recv()

        @pl.when(has_north)
        def _():
            row_copy(step, part, 0).wait_recv()

        @pl.when(has_south)
        def _():
            row_copy(step, part, 1).wait_recv()

    def wait_sent(step, part):
        for side in range(2):
            col_copy(step, part, side).wait_send()

        @pl.when(has_south)
        def _():
            row_copy(step, part, 0).wait_send()

        @pl.when(has_north)
        def _():
            row_copy(step, part, 1).wait_send()

    lanes = lax.broadcasted_iota(jnp.int32, (8, 128), 1)
    subs = lax.broadcasted_iota(jnp.int32, (8, 128), 0)
    zero = jnp.zeros((8, 128), F32)
    first_lane, last_lane = lanes == 0, lanes == 127
    first_sub, last_sub = subs == 0, subs == 7

    def keep_edges(step, block, slot, x, packs):
        row_out[step, 0, place_of(step, block), slot : slot + 1, :] = x[0:1]
        row_out[step, 1, place_of(step, block), slot : slot + 1, :] = x[7:8]
        here = lanes == slot
        return (
            jnp.where(here, jnp.broadcast_to(x[:, 0:1], (8, 128)), packs[0]),
            jnp.where(here, jnp.broadcast_to(x[:, 127:128], (8, 128)), packs[1]),
        )

    def put_packs(step, block, packs):
        col_out[step, 0, place_of(step, block)] = packs[0]
        col_out[step, 1, place_of(step, block)] = packs[1]

    def over_parts(step, body, carry, wait, send):
        size = part_size(step)

        def part_body(part, carry):
            if wait is not None:
                wait_part(wait, part)
            carry = lax.fori_loop(part * size, (part + 1) * size, body, carry)
            if send is not None:
                send_part(send, part)
            return carry

        return lax.fori_loop(0, blocks // size, part_body, carry)

    def level_at(ascending, block, i):
        count = block * UNROLL + i
        return count if ascending else levels - 1 - count

    lat_rows, lon_cells = adj_ref.shape[2:]
    cols = lat_rows * lon_cells
    loads[6].wait()
    column = column_ref[...]
    tile = column // cols
    cell = column - tile * cols
    lat_row = cell // lon_cells
    lane = cell - lat_row * lon_cells
    live = lax.broadcasted_iota(jnp.int32, (1, slots), 1) < count_ref[0]
    offset = jnp.where(tile >= b, tile - b, tile - b + n_lon)
    offset = jnp.where(live, offset, -1)
    which = lax.broadcasted_iota(jnp.int32, (n_lon, slots), 0)
    hits = jnp.where(which == offset, 1.0, 0.0).astype(F32)
    step = 256
    before = (
        lax.broadcasted_iota(jnp.int32, (step, step), 0)
        < lax.broadcasted_iota(jnp.int32, (step, step), 1)
    )
    upper = jnp.where(before, 1.0, 0.0).astype(BF16)
    base = jnp.zeros((n_lon, 1), F32)
    ranks = []
    for start in range(0, slots, step):
        part = hits[:, start : start + step]
        ahead = jnp.dot(part.astype(BF16), upper, preferred_element_type=F32) + base
        ranks.append(jnp.sum(part * ahead, axis=0, keepdims=True))
        base = base + jnp.sum(part, axis=1, keepdims=True)
    rank = jnp.concatenate(ranks, axis=1)
    half = jnp.zeros((1, slots), F32)
    for h in range(1, chunk):
        half = half + jnp.where(rank >= float(h * width), 1.0, 0.0)
    place = jnp.where(live, offset.astype(F32) * chunk + half, -1.0)
    within = rank - half * width
    loads[4].wait()
    loads[5].wait()
    wide = rows_ref[...].astype(F32)
    pay[0 : levels - 8, :] = wide[: levels - 8].astype(BF16)
    tail = jnp.concatenate(
        [
            retrieved_ref[...].astype(F32),
            lat_row.astype(F32),
            lane.astype(F32),
            jnp.zeros((8 - tracers - 2, slots), F32),
        ],
        axis=0,
    )
    pay[levels - 8 : levels + 8, :] = jnp.concatenate([wide[levels - 8 :], tail], axis=0).astype(BF16)
    rows16 = lax.broadcasted_iota(jnp.int32, (GROUP, slots), 0)
    column_of = jnp.where(rows16 == 0, jnp.broadcast_to(within, (GROUP, slots)), 0.0).astype(BF16)
    spread_first = jnp.where(
        lax.broadcasted_iota(jnp.int32, (GROUP, 128), 0) == 0, 1.0, 0.0
    ).astype(BF16)
    turned = lax.dot_general(column_of, spread_first, TN, preferred_element_type=F32)
    slot_of = lax.broadcasted_iota(jnp.int32, (1, 128), 1).astype(F32)
    for h in range(width // 128):
        weights[:, h * 128 : (h + 1) * 128] = jnp.where(
            turned == slot_of + float(h * 128), 1.0, 0.0
        ).astype(BF16)

    for n in (0, 1, 7, 8):
        loads[n].wait()
    station_cell, station_misfit = cell_ref[...], misfit_ref[...]
    for t in range(tracers):
        spot = subs * 128 + lanes
        add = zero
        for s in range(cell_ref.shape[1]):
            at = jnp.broadcast_to(station_cell[:, s : s + 1], (8, 128))
            term = jnp.broadcast_to(station_misfit[t : t + 1, s : s + 1], (8, 128))
            add = add + jnp.where(spot == at, term, 0.0)
        adj_ref[t, 0] = adj_ref[t, 0] + add
    kpad[0] = zero

    def start_body(block, carry):
        packs = (zero, zero)
        for i in range(UNROLL):
            level = block * UNROLL + i
            for t in range(tracers):
                packs = keep_edges(0, block, i * tracers + t, adj_ref[t, level], packs)
        put_packs(0, block, packs)
        return carry

    lax.fori_loop(0, blocks, start_body, 0)
    pl.semaphore_wait(barrier, n_lon + 1)
    for side in range(2):
        row_out[1, side, 0] = jnp.zeros(row_out.shape[3:], F32)
        col_out[1, side, 0] = zero

    def send_first(part, carry):
        send_part(0, part)
        return carry

    lax.fori_loop(0, PARTS, send_first, 0)

    several = max(1, 4 // chunk)

    def pack_body(turn, carry):
        picks = []
        for i in range(several * chunk):
            here = (turn * (several * chunk) + i).astype(F32)
            mask = jnp.where(place == here, 1.0, 0.0).astype(BF16)
            picks.append(pay[...] * mask)
        stacked = jnp.concatenate(picks, axis=0)
        total = jnp.dot(stacked, weights[...], preferred_element_type=F32).astype(BF16)
        for i in range(several):
            o = turn * several + i
            for h in range(chunk):
                at = (i * chunk + h) * height
                packed[o, :, h * width : (h + 1) * width] = total[at : at + height]

            @pl.when(o > 0)
            def _():
                for g in range(EARLY):
                    route_copy(o, g).start()

        return carry

    lax.fori_loop(0, n_lon // several, pack_body, 0)
    recv[:, 0:cap] = packed[0]
    send_group(EARLY)

    def factor_body(block, carry):
        for i in range(UNROLL):
            new = []
            for d in range(2):
                level = level_at(d == 0, block, i)
                below, above = kpad[level], kpad[level + 1]
                back, ahead = (below, above) if d == 0 else (above, below)
                inverse = 1.0 / (1.0 + below + above - back * back * carry[d])
                fac[d, 0, level] = inverse
                fac[d, 1, level] = back * inverse
                fac[d, 2, level] = ahead * inverse
                new.append(inverse)
            carry = tuple(new)
        return carry

    lax.fori_loop(0, blocks, factor_body, (zero, zero))

    def sweep_of(step, ascending, fetch):
        d = 0 if ascending else 1

        def sweep(block, carry):
            ys = list(carry)
            spot = place_of(step, block)
            col_e, col_w = col_in[step, 0, spot], col_in[step, 1, spot]
            for i in range(UNROLL):
                level = level_at(ascending, block, i)
                u, v = u_ref[level], v_ref[level]
                inverse, back = fac[d, 0, level], fac[d, 1, level]
                up, vp = jnp.maximum(u, 0.0), jnp.maximum(v, 0.0)
                un, vn = jnp.maximum(-u, 0.0), jnp.maximum(-v, 0.0)
                own = 1.0 - (up + un) - (vp + vn)
                for t in range(tracers):
                    slot = i * tracers + t
                    c = fetch(level, t)
                    e = jnp.where(
                        last_lane, pltpu.roll(col_e, 127 - slot, 1), pltpu.roll(c, 127, 1)
                    )
                    w = jnp.where(
                        first_lane, pltpu.roll(col_w, (128 - slot) % 128, 1), pltpu.roll(c, 1, 1)
                    )
                    row_n = jnp.broadcast_to(row_in[step, 0, spot, slot : slot + 1, :], (8, 128))
                    row_s = jnp.broadcast_to(row_in[step, 1, spot, slot : slot + 1, :], (8, 128))
                    n = jnp.where(last_sub, row_n, pltpu.roll(c, 7, 0))
                    s = jnp.where(first_sub, row_s, pltpu.roll(c, 1, 0))
                    q = (own * c + up * e) + (un * w) + (vp * n + vn * s)
                    y = q * inverse + back * ys[t]
                    y_buf[level, t] = y
                    ys[t] = y
            return tuple(ys)

        return sweep

    def substitute_of(step, ascending, emit, send):
        d = 0 if ascending else 1

        def substitute(block, carry):
            xs = list(carry)
            packs = (zero, zero)
            for i in range(UNROLL):
                level = level_at(not ascending, block, i)
                ahead = fac[d, 2, level]
                for t in range(tracers):
                    x = y_buf[level, t] + ahead * xs[t]
                    xs[t] = x
                    emit(level, t, x)
                    if send is not None:
                        packs = keep_edges(send, block, i * tracers + t, x, packs)
            if send is not None:
                put_packs(send, block, packs)
            return tuple(xs)

        return substitute

    def to_field(level, t, x):
        field[level, t] = x

    def to_out(level, t, x):
        out_ref[t, level] = x

    @pl.when(jnp.logical_not(has_north))
    def _():
        for step in range(3):
            row_in[step, 0] = jnp.zeros(row_in.shape[2:], F32)

    @pl.when(jnp.logical_not(has_south))
    def _():
        for step in range(3):
            row_in[step, 1] = jnp.zeros(row_in.shape[2:], F32)

    def from_field(level, t):
        return field[level, t]

    def from_input(level, t):
        return adj_ref[t, level]

    none = (zero,) * tracers
    loads[2].wait()
    loads[3].wait()
    over_parts(0, sweep_of(0, True, from_input), none, 0, None)
    send_group(EARLY + 1)
    over_parts(0, substitute_of(0, True, to_field, None), none, None, None)

    total_slots = n_lon * cap
    piece = min(512, total_slots)

    chosen_row = lax.broadcasted_iota(jnp.int32, (GROUP, (tracers + 1) * 128), 0) - (GROUP - 8)
    chosen_block = lax.broadcasted_iota(jnp.int32, (GROUP, (tracers + 1) * 128), 1) // 128
    wanted = jnp.where(chosen_block == tracers, tracers + 1, chosen_block)
    chosen = jnp.where(chosen_row == wanted, 1.0, 0.0).astype(BF16)
    lane_at = lax.broadcasted_iota(jnp.int32, (1, 128), 1).astype(F32)

    def prepare(n, carry):
        here = pl.ds(pl.multiple_of(n * piece, 128), piece)
        raw = recv[height - GROUP : height, here]
        meta = raw.astype(F32)
        turned = lax.dot_general(raw, chosen, TN, preferred_element_type=F32)
        hit = turned[:, tracers * 128 :] == lane_at
        for t in range(tracers):
            spread[here, t * 128 : (t + 1) * 128] = jnp.where(
                hit, turned[:, t * 128 : (t + 1) * 128], 0.0
            ).astype(BF16)
        row_of = meta[GROUP - 8 + tracers : GROUP - 7 + tracers]
        for r in range(8):
            mask = jnp.where(row_of == r, 1.0, 0.0).astype(BF16)
            masks[r, :, here] = jnp.broadcast_to(mask, (GROUP, piece))
        return carry

    sweep_1 = sweep_of(1, False, from_field)

    def group_edge(g):
        return jnp.maximum(g * (GROUP // UNROLL) - 1, 0)

    def group_body(g, ys):
        def arrived(o, carry):
            route_copy(o, g).wait_recv()
            return carry

        lax.fori_loop(1, n_lon, arrived, 0)

        @pl.when(g + EARLY + 2 < groups)
        def _():
            send_group(g + EARLY + 2)

        @pl.when(g == 0)
        def _():
            lax.fori_loop(0, total_slots // piece, prepare, 0)

        data = recv[group_rows(g), :]
        for r in range(8):
            left[r * GROUP : (r + 1) * GROUP, :] = data * masks[r]
        acc_all = jnp.dot(left[...], spread[...], preferred_element_type=F32)
        for t in range(tracers):
            acc[t] = acc_all[:, t * 128 : (t + 1) * 128]

        def inject_body(block, carry):
            packs = (zero, zero)
            for i in range(UNROLL):
                level = level_at(False, block, i)
                row = level - (levels + 8 - (g + 1) * GROUP)
                for t in range(tracers):
                    x = field[level, t] + acc[t, pl.ds(row, 8, GROUP), :]
                    field[level, t] = x
                    packs = keep_edges(1, block, i * tracers + t, x, packs)
            put_packs(1, block, packs)
            return carry

        lax.fori_loop(group_edge(g), group_edge(g + 1), inject_body, 0)
        send_part(1, g)

        @pl.when(g > 0)
        def _():
            wait_part(1, g - 1)

        return lax.fori_loop(group_edge(g - 1), group_edge(g), sweep_1, ys)

    ys = lax.fori_loop(0, groups, group_body, none)
    wait_part(1, groups - 1)
    lax.fori_loop(group_edge(groups - 1), group_edge(groups), sweep_1, ys)
    over_parts(0, substitute_of(1, False, to_field, 2), none, None, 2)

    over_parts(2, sweep_of(2, True, from_field), none, 2, None)
    last = substitute_of(2, True, to_out, None)
    size = part_size(2)

    def store(part):
        some = pl.ds(levels - (part + 1) * size * UNROLL, size * UNROLL)
        return pltpu.make_async_copy(out_ref.at[:, some], out_hbm.at[:, some], store_sem.at[part])

    def final(part, carry):
        carry = lax.fori_loop(part * size, (part + 1) * size, last, carry)
        store(part).start()
        return carry

    lax.fori_loop(0, PARTS, final, none)

    def route_sent(o, carry):
        for g in range(groups):
            route_copy(o, g).wait_send()
        return carry

    lax.fori_loop(1, n_lon, route_sent, 0)
    for step in range(3):

        def sent(part, carry, step=step):
            wait_sent(step, part)
            return carry

        lax.fori_loop(0, groups if step == 1 else PARTS, sent, 0)

    def stored(part, carry):
        store(part).wait()
        return carry

    lax.fori_loop(0, PARTS, stored, 0)


def body(
    n_lat, n_lon,
    adjoint_in, wind_u, wind_v, diffusion, kernel_rows, retrieval_misfit,
    retrieval_columns, retrieval_counts, station_cells, station_misfit,
):
    tracers, levels, lat_rows, lon_cells = adjoint_in.shape
    cols = lat_rows * lon_cells
    slots = kernel_rows.shape[1]
    cap = 2 * slots // n_lon
    width = min(cap, 256)
    height = levels + 8
    any_space = pl.BlockSpec(memory_space=pl.ANY)
    hbm = pl.BlockSpec(memory_space=pltpu.HBM)
    stations = station_cells.shape[0]
    smem = pl.BlockSpec(memory_space=pltpu.SMEM)
    groups = height // GROUP
    blocks = levels // UNROLL
    edge = UNROLL * tracers
    return pl.pallas_call(
        functools.partial(transport_kernel, n_lat, n_lon),
        out_shape=jax.ShapeDtypeStruct(adjoint_in.shape, F32),
        in_specs=[hbm] * 7 + [smem] + [hbm] * 2,
        out_specs=any_space,
        scratch_shapes=[
            pltpu.VMEM(adjoint_in.shape, F32),
            pltpu.VMEM(wind_u.shape, F32),
            pltpu.VMEM(wind_v.shape, F32),
            pltpu.VMEM(kernel_rows.shape, BF16),
            pltpu.VMEM(retrieval_misfit.shape, BF16),
            pltpu.VMEM((1, slots), jnp.int32),
            pltpu.VMEM((1, stations), jnp.int32),
            pltpu.VMEM(station_misfit.shape, F32),
            pltpu.VMEM(adjoint_in.shape, F32),
            pltpu.VMEM((levels, tracers, 8, 128), F32),
            pltpu.VMEM((levels, tracers, 8, 128), F32),
            pltpu.VMEM((levels + 1, 8, 128), F32),
            pltpu.VMEM((2, 3, levels, 8, 128), F32),
            pltpu.VMEM((tracers, 8 * GROUP, 128), F32),
            pltpu.VMEM((height, slots), BF16),
            pltpu.VMEM((n_lon, height, cap), BF16),
            pltpu.VMEM((height, n_lon * cap), BF16),
            pltpu.VMEM((slots, width), BF16),
            pltpu.VMEM((n_lon * cap, tracers * 128), BF16),
            pltpu.VMEM((8, GROUP, n_lon * cap), BF16),
            pltpu.VMEM((8 * GROUP, n_lon * cap), BF16),
            pltpu.VMEM((3, 2, blocks + 1, edge, 128), F32),
            pltpu.VMEM((3, 2, blocks + 1, edge, 128), F32),
            pltpu.VMEM((3, 2, blocks + 1, 8, 128), F32),
            pltpu.VMEM((3, 2, blocks + 1, 8, 128), F32),
            pltpu.SemaphoreType.DMA((9,)),
            pltpu.SemaphoreType.DMA((PARTS,)),
            pltpu.SemaphoreType.DMA((n_lon, groups)),
            pltpu.SemaphoreType.DMA((n_lon, groups)),
            pltpu.SemaphoreType.DMA((3, max(groups, PARTS), 4)),
            pltpu.SemaphoreType.DMA((3, max(groups, PARTS), 4)),
        ],
        compiler_params=pltpu.CompilerParams(
            collective_id=0, has_side_effects=True, vmem_limit_bytes=60 * 2**20
        ),
        name="transport",
    )(
        adjoint_in, wind_u, wind_v, diffusion, kernel_rows, retrieval_misfit,
        retrieval_columns.reshape(1, slots), retrieval_counts, station_cells.reshape(1, stations), station_misfit,
    )


def solution(mesh):
    return jax.shard_map(
        functools.partial(body, mesh.shape["lat"], mesh.shape["lon"]),
        mesh=mesh,
        in_specs=(
            P(None, None, "lat", "lon"),
            P(None, "lat", "lon"),
            P(None, "lat", "lon"),
            P(None, "lat", "lon"),
            P(None, ("lat", "lon")),
            P(None, ("lat", "lon")),
            P(("lat", "lon")),
            P(("lat", "lon")),
            P(("lat", "lon")),
            P(None, ("lat", "lon")),
        ),
        out_specs=P(None, None, "lat", "lon"),
        check_vma=False,
    )
```
